32 devices in a mesh: grp: 2 (over x), aux: 16 (over z, y, core).
Axes of the slice: x: 2, y: 2, z: 4, core: 2. Of those that a mesh axis runs over, the one named last changes fastest.
Arguments:
- three_index: bfloat16 [128, 256, 256], P('grp', 'aux'), parts along dimension 0, may hold values from -6 to 6
- fit_metric: float32 [512, 16], P(('grp', 'aux')), parts along dimension 0, as said below
- fit_blocks: int32 [128, 12], P('grp'), parts along dimension 0, may hold values from 0 to 15, as said below
- domains: int32 [128, 256], P('grp'), parts along dimension 0, may hold values from 0 to 19999
- occ_energy: float32 [128], P('grp'), parts along dimension 0, may hold values from -1.5 to -0.3
- virt_energy: float32 [40000], P('grp'), parts along dimension 0, may hold values from 0.2 to 3
- owner_map: int32 [128], P('grp'), parts along dimension 0, may hold values from 0 to 63, as said below
- partners: int32 [32, 8], P('grp'), parts along dimension 0, may hold values from 0 to 63, as said below
Outputs:
- slab_energy: float32 [128, 4], P(('grp', 'aux')), parts along dimension 0
- partner_energy: float32 [128, 8], P(('grp', 'aux')), parts along dimension 0
- energy_per_orbital: float32 [2], P('grp'), parts along dimension 0
The draws below stay inside these ranges and needn't reach their ends.
There are 2 independent parts, one for each index of `grp`. The reference program is written for one: setup_inputs(seed, part) draws one part's arguments, and reference() takes and returns one part's arrays. A program takes and returns all parts, laid end to end along the dimension named above; each array names one. Nothing has to cross between parts.
Inputs may be any that keep to these rules, and one draw needn't show every extreme that they name: `owner_map`: A permutation of the occupied orbitals. `partners`: each row lists 8 different orbitals, none of them held by that slab. `fit_blocks`: each row lists 12 different auxiliary blocks. `fit_metric`: each block of 16 consecutive rows holds that block's weights.
All inputs are finite; a program needn't handle non-finite values.
Results may differ from the reference program's by a relative error of at most 0.0003.
Values may be sent and summed in bfloat16 or wider, within the bound.
A program may use at most 128 MiB of HBM per device.

```python
import jax
import jax.numpy as jnp
from jax import lax

OCC_DEV = 4
NPART = 8
DOM = 256
NAUX_DEV = 16
NVIRT = 20000
OCC = 64
NAUX = 256
FITB = 12
N_AUX = 16


def shared_order(key):
    return jax.random.permutation(jax.random.fold_in(key, 101), OCC).astype(jnp.int32)


def draw_owner_map(key, part):
    order = shared_order(key)
    return order


def draw_partners(key, part):
    order = shared_order(key)
    key = jax.random.fold_in(key, 2)
    keys = jax.random.split(key, N_AUX)
    offsets = jax.vmap(lambda single: jax.random.permutation(single, OCC - OCC_DEV)[:NPART])(keys)
    starts = (jnp.arange(N_AUX, dtype=jnp.int32) * OCC_DEV + OCC_DEV)[:, None]
    return order[(starts + offsets.astype(jnp.int32)) % OCC].astype(jnp.int32)


def draw_fit_blocks(key, part):
    key = jax.random.fold_in(key, 3)
    keys = jax.random.split(key, OCC)
    return jax.vmap(lambda single: jax.random.permutation(single, N_AUX)[:FITB])(keys).astype(jnp.int32)


def draw_fit_metric(key, part):
    key = jax.random.fold_in(key, 4)
    first = jax.random.fold_in(key, 0)
    noise = jax.random.normal(first, (NAUX, NAUX_DEV), jnp.float32) * 0.15
    unit = (jnp.arange(NAUX)[:, None] % NAUX_DEV == jnp.arange(NAUX_DEV)[None, :]).astype(jnp.float32)
    factor = (DOM * (FITB * NAUX_DEV) ** 0.5) ** (-0.5)
    return ((unit + noise) * factor).astype(jnp.float32)


def set_ends(entries, own_key, low, top_value):
    longest = entries.shape.index(max(entries.shape))
    spots = []
    for shift in (0, 1):
        where = [jax.random.randint(jax.random.fold_in(own_key, axis), (), 0, length) for axis, length in enumerate(entries.shape)]
        where[longest] = (where[longest] + shift) % entries.shape[longest]
        spots.append(tuple(where))
    return entries.at[spots[0]].set(low).at[spots[1]].set(top_value)


def levels(rng, dims, cuts, low, high):
    def one(dim, shards_of):
        draws = jax.random.uniform(jax.random.fold_in(jax.random.fold_in(rng, 6), dim), (shards_of,), jnp.float32, low / len(cuts), high / len(cuts))
        return jnp.repeat(jnp.exp(draws), dims[dim] // shards_of).reshape((-1,) + (1,) * (len(dims) - dim - 1))

    gain = one(*cuts[0])
    for cut in cuts[1:]:
        gain = gain * one(*cut)
    return gain


def bell_draw(stream_key, dims, deviation, bound, pieces=(), kind=jnp.bfloat16):
    level = levels(stream_key, dims, pieces, -0.22, 0.18) if pieces else 1.0
    array = jax.random.normal(stream_key, dims, jnp.float32) * deviation * level
    return jnp.minimum(jnp.maximum(array, -bound), bound).astype(kind)


def setup_inputs(seed: int = 0, part: int = 0) -> dict:
    streams_of = jax.random.split(jax.random.key(seed), 9)
    part_splits = jax.random.split(jax.random.fold_in(streams_of[8], part), 9)
    return {
        "three_index": bell_draw(part_splits[0], (OCC, NAUX, DOM), 1.0, 6.0, ((1, 16),)),
        "fit_metric": draw_fit_metric(jax.random.fold_in(jax.random.fold_in(streams_of[8], part), 71), part),
        "fit_blocks": draw_fit_blocks(jax.random.fold_in(jax.random.fold_in(streams_of[8], part), 71), part),
        "domains": set_ends(jax.random.randint(part_splits[3], (OCC, DOM), 0, NVIRT), jax.random.fold_in(part_splits[3], 1), 0, NVIRT - 1).astype(jnp.int32),
        "occ_energy": jnp.clip(jax.random.uniform(part_splits[4], (OCC,), jnp.float32, -1.5, -0.3), -1.5, -0.3),
        "virt_energy": jnp.clip(jax.random.uniform(part_splits[5], (NVIRT,), jnp.float32, 0.2, 3.0), 0.2, 3.0),
        "owner_map": draw_owner_map(jax.random.fold_in(jax.random.fold_in(streams_of[8], part), 71), part),
        "partners": draw_partners(jax.random.fold_in(jax.random.fold_in(streams_of[8], part), 71), part),
    }


def pair_energy(left, right, left_ids, right_ids, row_mask, domains, occ_energy, virt_energy):
    masked = left * row_mask[:, :, None]
    coulomb = jnp.einsum("ipa,jpb->ijab", masked.astype(jnp.float32), right.astype(jnp.float32))
    left_gap = jnp.take(virt_energy, domains[left_ids], axis=0) - occ_energy[left_ids][:, None]
    right_gap = jnp.take(virt_energy, domains[right_ids], axis=0) - occ_energy[right_ids][:, None]
    divisor = left_gap[:, None, :, None] + right_gap[None, :, None, :]
    return -jnp.sum(coulomb * coulomb / divisor, axis=(2, 3))


def reference(three_index, fit_metric, fit_blocks, domains, occ_energy, virt_energy, owner_map, partners):
    weights = fit_metric.reshape(N_AUX, NAUX_DEV, NAUX_DEV)

    def fit_one(rows):
        blocks = rows.astype(jnp.float32).reshape(N_AUX, NAUX_DEV, DOM)
        done = jnp.einsum("npq,nqa->npa", weights, blocks, precision=lax.Precision.HIGHEST)
        return done.reshape(NAUX, DOM).astype(jnp.bfloat16)

    fitted = lax.map(fit_one, three_index)

    def one_slab(slab_index):
        own_ids = lax.dynamic_slice_in_dim(owner_map, (slab_index * OCC_DEV).astype(jnp.int32), OCC_DEV)
        part_ids = partners[slab_index]
        own = fitted[own_ids]
        mates = fitted[part_ids]
        listed = fit_blocks[own_ids]
        hits = jnp.any(listed[:, :, None] == jnp.arange(N_AUX, dtype=jnp.int32)[None, None, :], axis=1)
        row_mask = jnp.repeat(hits.astype(jnp.bfloat16), NAUX_DEV, axis=1)
        inside = pair_energy(own, own, own_ids, own_ids, row_mask, domains, occ_energy, virt_energy)
        outside = pair_energy(own, mates, own_ids, part_ids, row_mask, domains, occ_energy, virt_energy)
        return inside, outside

    inside, outside = lax.map(one_slab, jnp.arange(N_AUX, dtype=jnp.int32))
    slab_energy = inside.reshape(OCC, OCC_DEV)
    partner_energy = outside.reshape(OCC, NPART)
    total = (jnp.sum(slab_energy) + jnp.sum(partner_energy)) / OCC
    return slab_energy, partner_energy, total.reshape(1)
```

```python
import functools

import jax
import jax.numpy as jnp
from jax import lax
from jax.experimental import pallas as pl
from jax.experimental.pallas import tpu as pltpu
from jax.sharding import PartitionSpec as P

HIGHEST = lax.Precision.HIGHEST
LANES = 128


def kernel(
    n, slab, npart,
    owner_ref, partners_ref, blocks_ref, occ_ref,
    three_ref, metric_ref, domains_ref, table_ref,
    out_ref,
    fitted, send, recv, inverse, left_t, gaps, sums, totals,
    send_sem, recv_sem, tot_send_sem, tot_recv_sem,
):
    me = lax.axis_index("aux")
    total_occ, rows, width = three_ref.shape
    width_p = n * rows
    joined = slab + npart
    order_start = max(n // 2 - 1, 0)

    def peer(step):
        return lax.rem(me + 1 + lax.rem(step + order_start, n - 1), n)

    def orbital(t, slot):
        return owner_ref[t * slab + slot] if slot < slab else partners_ref[t, slot - slab]

    barrier = pltpu.get_barrier_semaphore()

    def greet(step, carry):
        pl.semaphore_signal(
            barrier, inc=1, device_id={"aux": peer(step)}, device_id_type=pl.DeviceIdType.MESH
        )
        return carry

    lax.fori_loop(0, n - 1, greet, 0)

    group = 256 // rows
    side = group * rows
    tall = jnp.concatenate([metric_ref[...]] * group, axis=0)
    spread = (
        lax.broadcasted_iota(jnp.int32, (rows, side), 1) % rows
        == lax.broadcasted_iota(jnp.int32, (rows, side), 0)
    ).astype(jnp.float32)
    tiled = jnp.dot(tall, spread, precision=HIGHEST, preferred_element_type=jnp.float32)
    same = (
        lax.broadcasted_iota(jnp.int32, (side, side), 0) // rows
        == lax.broadcasted_iota(jnp.int32, (side, side), 1) // rows
    )
    weights = jnp.where(same, tiled, 0.0)
    first = weights.astype(jnp.bfloat16)
    rest = weights - first.astype(jnp.float32)
    second = rest.astype(jnp.bfloat16)
    third = (rest - second.astype(jnp.float32)).astype(jnp.bfloat16)

    def fit(g, carry):
        block = three_ref[pl.ds(g * group, group)].reshape(side, width)
        done = jnp.dot(third, block, preferred_element_type=jnp.float32)
        done += jnp.dot(second, block, preferred_element_type=jnp.float32)
        done += jnp.dot(first, block, preferred_element_type=jnp.float32)
        fitted[pl.ds(g * group, group)] = done.astype(jnp.bfloat16).reshape(group, rows, width)
        return carry

    lax.fori_loop(0, total_occ // group, fit, 0)

    pl.semaphore_wait(barrier, n - 1)

    def block_copy(target, source):
        return pltpu.make_async_remote_copy(
            src_ref=send.at[target], dst_ref=recv.at[source],
            send_sem=send_sem.at[target], recv_sem=recv_sem.at[source],
            device_id={"aux": target}, device_id_type=pl.DeviceIdType.MESH,
        )

    def pack(step, carry):
        t = peer(step)
        for slot in range(joined):
            send[t, slot] = fitted[orbital(t, slot)]
        block_copy(t, me).start()
        return carry

    lax.fori_loop(0, n - 1, pack, 0)
    for slot in range(joined):
        recv[me, slot] = fitted[orbital(me, slot)]

    depth = table_ref.shape[0]
    by_lane = table_ref[...].T
    for slot in range(joined):
        one = orbital(me, slot)
        index = domains_ref[pl.ds(one, 1), :]
        high = index // LANES
        low = index - high * LANES
        pick = (lax.broadcasted_iota(jnp.int32, (depth, width), 0) == high).astype(jnp.float32)
        values = jnp.dot(by_lane, pick, precision=HIGHEST, preferred_element_type=jnp.float32)
        chosen = jnp.where(lax.broadcasted_iota(jnp.int32, (LANES, width), 0) == low, values, 0.0)
        gaps[pl.ds(slot, 1), :] = jnp.sum(chosen, axis=0, keepdims=True) - occ_ref[one]
    for i in range(slab):
        down = jnp.broadcast_to(gaps[pl.ds(i, 1), :], (width, width)).T

        def invert(j, carry, i=i, down=down):
            inverse[i, j] = 1.0 / (down + gaps[pl.ds(j, 1), :])
            return carry

        lax.fori_loop(0, joined, invert, 0)
    sums[...] = jnp.zeros_like(sums)

    def arrive(step, carry):
        source = peer(step)
        block_copy(source, source).wait_recv()
        return carry

    lax.fori_loop(0, n - 1, arrive, 0)

    block_of = lax.broadcasted_iota(jnp.int32, (1, width_p), 1) // rows
    for i in range(slab):
        one = orbital(me, i)

        def hit(f, found, one=one):
            return jnp.where(block_of == blocks_ref[one, f], 1.0, found)

        mask = lax.fori_loop(
            0, blocks_ref.shape[1], hit, jnp.zeros((1, width_p), jnp.float32), unroll=width_p <= 512
        )
        turned = recv[:, i].reshape(width_p, width).astype(jnp.float32).T
        left_t[i] = (turned * mask).astype(jnp.bfloat16)

    def pairs(i, carry):
        left = left_t[i]
        for j in range(joined):
            right = recv[:, j].reshape(width_p, width)
            coulomb = jnp.dot(left, right, preferred_element_type=jnp.float32)
            terms = coulomb * coulomb * inverse[i, j]
            sums[i, pl.ds(j, 1), :] = jnp.sum(terms, axis=0, keepdims=True)
        return carry

    lax.fori_loop(0, slab, pairs, 0)

    ones = jnp.ones((8, width), jnp.float32)
    energies = [
        -lax.dot_general(
            ones, sums[i], (((1,), (1,)), ((), ())),
            precision=HIGHEST, preferred_element_type=jnp.float32,
        )[0:1]
        for i in range(slab)
    ]
    pad = jnp.zeros((8 - slab, LANES), jnp.float32)
    table = jnp.concatenate(energies + [pad], axis=0)
    totals[me] = table

    def total_copy(target, source):
        return pltpu.make_async_remote_copy(
            src_ref=totals.at[me], dst_ref=totals.at[source],
            send_sem=tot_send_sem.at[target], recv_sem=tot_recv_sem.at[source],
            device_id={"aux": target}, device_id_type=pl.DeviceIdType.MESH,
        )

    def give(step, carry):
        total_copy(peer(step), me).start()
        return carry

    lax.fori_loop(0, n - 1, give, 0)

    def take(step, carry):
        source = peer(step)
        total_copy(source, source).wait_recv()
        return carry

    lax.fori_loop(0, n - 1, take, 0)
    whole = jnp.sum(jnp.sum(totals[...], axis=0), axis=(0, 1), keepdims=True) / total_occ
    last = lax.broadcasted_iota(jnp.int32, (8, LANES), 0) == slab
    out_ref[...] = jnp.where(last, whole, table)

    def finish(step, carry):
        t = peer(step)
        block_copy(t, me).wait_send()
        total_copy(t, me).wait_send()
        return carry

    lax.fori_loop(0, n - 1, finish, 0)


def per_device(
    three_index, fit_metric, fit_blocks, domains, occ_energy, virt_energy, owner_map, partners
):
    n = lax.axis_size("aux")
    total_occ, rows, width = three_index.shape
    slab = total_occ // n
    npart = partners.shape[1]
    joined = slab + npart
    chunk = 8 * LANES
    length = -(-virt_energy.shape[0] // chunk) * chunk
    table = jnp.pad(virt_energy, (0, length - virt_energy.shape[0])).reshape(-1, LANES)
    smem = pl.BlockSpec(memory_space=pltpu.SMEM)
    vmem = pl.BlockSpec(memory_space=pltpu.VMEM)
    out = pl.pallas_call(
        functools.partial(kernel, n, slab, npart),
        out_shape=jax.ShapeDtypeStruct((8, LANES), jnp.float32),
        in_specs=[smem] * 4 + [vmem] * 4,
        out_specs=vmem,
        scratch_shapes=[
            pltpu.VMEM((total_occ, rows, width), jnp.bfloat16),
            pltpu.VMEM((n, joined, rows, width), jnp.bfloat16),
            pltpu.VMEM((n, joined, rows, width), jnp.bfloat16),
            pltpu.VMEM((slab, joined, width, width), jnp.float32),
            pltpu.VMEM((slab, width, n * rows), jnp.bfloat16),
            pltpu.VMEM((-(-joined // 8) * 8, width), jnp.float32),
            pltpu.VMEM((slab, LANES, width), jnp.float32),
            pltpu.VMEM((n, 8, LANES), jnp.float32),
            pltpu.SemaphoreType.DMA((n,)),
            pltpu.SemaphoreType.DMA((n,)),
            pltpu.SemaphoreType.DMA((n,)),
            pltpu.SemaphoreType.DMA((n,)),
        ],
        compiler_params=pltpu.CompilerParams(
            collective_id=0, has_side_effects=True, vmem_limit_bytes=56 * 1024 * 1024
        ),
    )(owner_map, partners, fit_blocks, occ_energy, three_index, fit_metric, domains, table)
    return out[:slab, :slab], out[:slab, slab:joined], out[slab, :1]


def solution(mesh):
    in_specs = (
        P("grp", "aux", None),
        P(("grp", "aux"), None),
        P("grp", None),
        P("grp", None),
        P("grp"),
        P("grp"),
        P("grp"),
        P("grp", None),
    )
    out_specs = (P(("grp", "aux"), None), P(("grp", "aux"), None), P("grp"))
    return jax.shard_map(
        per_device, mesh=mesh, in_specs=in_specs, out_specs=out_specs, check_vma=False
    )
```

```python
import functools

import jax
import jax.numpy as jnp
from jax import lax
from jax.experimental import pallas as pl
from jax.experimental.pallas import tpu as pltpu
from jax.sharding import PartitionSpec as P

HIGHEST = lax.Precision.HIGHEST
LANES = 128


def kernel(
    n, slab, npart,
    owner_ref, partners_ref, blocks_ref, occ_ref,
    three_ref, metric_ref, domains_ref, virt_ref,
    out_ref,
    fitted, send, recv, table_ref, inverse, left_t, gaps, sums, totals,
    send_sem, recv_sem, tot_send_sem, tot_recv_sem,
):
    me = lax.axis_index("aux")
    total_occ, rows, width = three_ref.shape
    width_p = n * rows
    joined = slab + npart
    order_start = max(n // 2 - 1, 0)

    def peer(step):
        return lax.rem(me + 1 + lax.rem(step + order_start, n - 1), n)

    def orbital(t, slot):
        return owner_ref[t * slab + slot] if slot < slab else partners_ref[slot - slab, t]

    barrier = pltpu.get_barrier_semaphore()

    def greet(step, carry):
        pl.semaphore_signal(
            barrier, inc=1, device_id={"aux": peer(step)}, device_id_type=pl.DeviceIdType.MESH
        )
        return carry

    lax.fori_loop(0, n - 1, greet, 0)

    group = 256 // rows
    side = group * rows
    tall = jnp.concatenate([metric_ref[...]] * group, axis=0)
    spread = (
        lax.broadcasted_iota(jnp.int32, (rows, side), 1) % rows
        == lax.broadcasted_iota(jnp.int32, (rows, side), 0)
    ).astype(jnp.float32)
    tiled = jnp.dot(tall, spread, precision=HIGHEST, preferred_element_type=jnp.float32)
    same = (
        lax.broadcasted_iota(jnp.int32, (side, side), 0) // rows
        == lax.broadcasted_iota(jnp.int32, (side, side), 1) // rows
    )
    weights = jnp.where(same, tiled, 0.0)
    first = weights.astype(jnp.bfloat16)
    rest = weights - first.astype(jnp.float32)
    second = rest.astype(jnp.bfloat16)
    third = (rest - second.astype(jnp.float32)).astype(jnp.bfloat16)

    def fit(g, carry):
        block = three_ref[pl.ds(g * group, group)].reshape(side, width)
        done = jnp.dot(third, block, preferred_element_type=jnp.float32)
        done += jnp.dot(second, block, preferred_element_type=jnp.float32)
        done += jnp.dot(first, block, preferred_element_type=jnp.float32)
        fitted[pl.ds(g * group, group)] = done.astype(jnp.bfloat16).reshape(group, rows, width)
        return carry

    lax.fori_loop(0, total_occ // group, fit, 0)

    pl.semaphore_wait(barrier, n - 1)

    def block_copy(target, source):
        return pltpu.make_async_remote_copy(
            src_ref=send.at[target], dst_ref=recv.at[source],
            send_sem=send_sem.at[target], recv_sem=recv_sem.at[source],
            device_id={"aux": target}, device_id_type=pl.DeviceIdType.MESH,
        )

    def pack(step, carry):
        t = peer(step)
        for slot in range(joined):
            send[t, slot] = fitted[orbital(t, slot)]
        block_copy(t, me).start()
        return carry

    lax.fori_loop(0, n - 1, pack, 0)
    for slot in range(joined):
        recv[me, slot] = fitted[orbital(me, slot)]

    depth = table_ref.shape[0]
    n_virt = virt_ref.shape[0]
    full = n_virt // LANES
    table_ref[...] = jnp.zeros_like(table_ref)
    for row in range(full):
        table_ref[row, :] = virt_ref[pl.ds(row * LANES, LANES)]
    if n_virt % LANES:
        table_ref[full, 0 : n_virt % LANES] = virt_ref[pl.ds(full * LANES, n_virt % LANES)]
    by_lane = table_ref[...].T
    for slot in range(joined):
        one = orbital(me, slot)
        index = domains_ref[pl.ds(one, 1), :]
        high = index // LANES
        low = index - high * LANES
        pick = (lax.broadcasted_iota(jnp.int32, (depth, width), 0) == high).astype(jnp.float32)
        values = jnp.dot(by_lane, pick, precision=HIGHEST, preferred_element_type=jnp.float32)
        chosen = jnp.where(lax.broadcasted_iota(jnp.int32, (LANES, width), 0) == low, values, 0.0)
        gaps[pl.ds(slot, 1), :] = jnp.sum(chosen, axis=0, keepdims=True) - occ_ref[one]
    for i in range(slab):
        down = jnp.broadcast_to(gaps[pl.ds(i, 1), :], (width, width)).T

        def invert(j, carry, i=i, down=down):
            inverse[i, j] = 1.0 / (down + gaps[pl.ds(j, 1), :])
            return carry

        lax.fori_loop(0, joined, invert, 0)
    sums[...] = jnp.zeros_like(sums)

    def arrive(step, carry):
        source = peer(step)
        block_copy(source, source).wait_recv()
        return carry

    lax.fori_loop(0, n - 1, arrive, 0)

    block_of = lax.broadcasted_iota(jnp.int32, (1, width_p), 1) // rows
    for i in range(slab):
        one = orbital(me, i)

        def hit(f, found, one=one):
            return jnp.where(block_of == blocks_ref[f, one], 1.0, found)

        mask = lax.fori_loop(
            0, blocks_ref.shape[0], hit, jnp.zeros((1, width_p), jnp.float32), unroll=width_p <= 512
        )
        turned = recv[:, i].reshape(width_p, width).astype(jnp.float32).T
        left_t[i] = (turned * mask).astype(jnp.bfloat16)

    def pairs(i, carry):
        left = left_t[i]
        for j in range(joined):
            right = recv[:, j].reshape(width_p, width)
            coulomb = jnp.dot(left, right, preferred_element_type=jnp.float32)
            terms = coulomb * coulomb * inverse[i, j]
            sums[i, pl.ds(j, 1), :] = jnp.sum(terms, axis=0, keepdims=True)
        return carry

    lax.fori_loop(0, slab, pairs, 0)

    ones = jnp.ones((8, width), jnp.float32)
    energies = [
        -lax.dot_general(
            ones, sums[i], (((1,), (1,)), ((), ())),
            precision=HIGHEST, preferred_element_type=jnp.float32,
        )[0:1]
        for i in range(slab)
    ]
    pad = jnp.zeros((8 - slab, LANES), jnp.float32)
    table = jnp.concatenate(energies + [pad], axis=0)
    totals[me] = table

    def total_copy(target, source):
        return pltpu.make_async_remote_copy(
            src_ref=totals.at[me], dst_ref=totals.at[source],
            send_sem=tot_send_sem.at[target], recv_sem=tot_recv_sem.at[source],
            device_id={"aux": target}, device_id_type=pl.DeviceIdType.MESH,
        )

    def give(step, carry):
        total_copy(peer(step), me).start()
        return carry

    lax.fori_loop(0, n - 1, give, 0)

    def take(step, carry):
        source = peer(step)
        total_copy(source, source).wait_recv()
        return carry

    lax.fori_loop(0, n - 1, take, 0)
    whole = jnp.sum(jnp.sum(totals[...], axis=0), axis=(0, 1), keepdims=True) / total_occ
    last = lax.broadcasted_iota(jnp.int32, (8, LANES), 0) == slab
    out_ref[...] = jnp.where(last, whole, table)

    def finish(step, carry):
        t = peer(step)
        block_copy(t, me).wait_send()
        total_copy(t, me).wait_send()
        return carry

    lax.fori_loop(0, n - 1, finish, 0)


def split_outputs(table_ref, slab_ref, partner_ref, total_ref):
    slab, npart = partner_ref.shape
    slab_ref[...] = table_ref[0:slab, 0:slab]
    partner_ref[...] = table_ref[0:slab, slab : slab + npart]
    total_ref[...] = table_ref[slab : slab + 1, 0:1]


def per_device(
    three_index, fit_metric, fit_blocks, domains, occ_energy, virt_energy, owner_map, partners
):
    n = lax.axis_size("aux")
    total_occ, rows, width = three_index.shape
    slab = total_occ // n
    npart = partners.shape[1]
    joined = slab + npart
    chunk = 8 * LANES
    depth = -(-virt_energy.shape[0] // chunk) * 8
    smem = pl.BlockSpec(memory_space=pltpu.SMEM)
    vmem = pl.BlockSpec(memory_space=pltpu.VMEM)
    out = pl.pallas_call(
        functools.partial(kernel, n, slab, npart),
        out_shape=jax.ShapeDtypeStruct((8, LANES), jnp.float32),
        in_specs=[smem] * 4 + [vmem] * 4,
        out_specs=vmem,
        scratch_shapes=[
            pltpu.VMEM((total_occ, rows, width), jnp.bfloat16),
            pltpu.VMEM((n, joined, rows, width), jnp.bfloat16),
            pltpu.VMEM((n, joined, rows, width), jnp.bfloat16),
            pltpu.VMEM((depth, LANES), jnp.float32),
            pltpu.VMEM((slab, joined, width, width), jnp.float32),
            pltpu.VMEM((slab, width, n * rows), jnp.bfloat16),
            pltpu.VMEM((-(-joined // 8) * 8, width), jnp.float32),
            pltpu.VMEM((slab, LANES, width), jnp.float32),
            pltpu.VMEM((n, 8, LANES), jnp.float32),
            pltpu.SemaphoreType.DMA((n,)),
            pltpu.SemaphoreType.DMA((n,)),
            pltpu.SemaphoreType.DMA((n,)),
            pltpu.SemaphoreType.DMA((n,)),
        ],
        compiler_params=pltpu.CompilerParams(
            collective_id=0, has_side_effects=True, vmem_limit_bytes=56 * 1024 * 1024
        ),
    )(
        owner_map, partners.T, fit_blocks.T, occ_energy, three_index, fit_metric, domains, virt_energy
    )
    slab_energy, partner_energy, total = pl.pallas_call(
        split_outputs,
        out_shape=(
            jax.ShapeDtypeStruct((slab, slab), jnp.float32),
            jax.ShapeDtypeStruct((slab, npart), jnp.float32),
            jax.ShapeDtypeStruct((1, 1), jnp.float32),
        ),
        in_specs=[vmem],
        out_specs=(vmem, vmem, vmem),
    )(out)
    return slab_energy, partner_energy, total.reshape(1)


def solution(mesh):
    in_specs = (
        P("grp", "aux", None),
        P(("grp", "aux"), None),
        P("grp", None),
        P("grp", None),
        P("grp"),
        P("grp"),
        P("grp"),
        P("grp", None),
    )
    out_specs = (P(("grp", "aux"), None), P(("grp", "aux"), None), P("grp"))
    return jax.shard_map(
        per_device, mesh=mesh, in_specs=in_specs, out_specs=out_specs, check_vma=False
    )
```

```python
import functools

import jax
import jax.numpy as jnp
from jax import lax
from jax.experimental import pallas as pl
from jax.experimental.pallas import tpu as pltpu
from jax.sharding import PartitionSpec as P

HIGHEST = lax.Precision.HIGHEST
LANES = 128


def kernel(
    n, slab, npart,
    owner_ref, partners_ref, blocks_ref, occ_ref,
    three_ref, metric_ref, domains_ref, virt_ref,
    out_ref,
    fitted, cross_a, cross_b, send, relay, recv, table_ref, inverse, left_t, gaps, sums, totals,
    cross_send_sem, cross_recv_sem, send_sem, relay_sem, recv_sem, tot_send_sem, tot_recv_sem,
):
    me = lax.axis_index("aux")
    total_occ, rows, width = three_ref.shape
    width_p = n * rows
    joined = slab + npart
    order_start = n // 2 - 1
    half = n // 2
    here = lax.rem(me, half)
    base = me - here
    across = lax.rem(me + half, n)
    crossed = (cross_a, cross_b)
    part = width // 2

    def near(step):
        return base + lax.rem(here + 1 + step, half)

    def peer(step):
        return lax.rem(me + 1 + lax.rem(step + order_start, n - 1), n)

    def orbital(t, slot):
        return owner_ref[t * slab + slot] if slot < slab else partners_ref[slot - slab, t]

    barrier = pltpu.get_barrier_semaphore()

    def greet(step, carry):
        pl.semaphore_signal(
            barrier, inc=1, device_id={"aux": peer(step)}, device_id_type=pl.DeviceIdType.MESH
        )
        return carry

    lax.fori_loop(0, n - 1, greet, 0)

    group = 256 // rows
    side = group * rows
    tall = jnp.concatenate([metric_ref[...]] * group, axis=0)
    spread = (
        lax.broadcasted_iota(jnp.int32, (rows, side), 1) % rows
        == lax.broadcasted_iota(jnp.int32, (rows, side), 0)
    ).astype(jnp.float32)
    tiled = jnp.dot(tall, spread, precision=HIGHEST, preferred_element_type=jnp.float32)
    same = (
        lax.broadcasted_iota(jnp.int32, (side, side), 0) // rows
        == lax.broadcasted_iota(jnp.int32, (side, side), 1) // rows
    )
    weights = jnp.where(same, tiled, 0.0)
    first = weights.astype(jnp.bfloat16)
    rest = weights - first.astype(jnp.float32)
    second = rest.astype(jnp.bfloat16)
    third = (rest - second.astype(jnp.float32)).astype(jnp.bfloat16)

    def fit(g, carry):
        block = three_ref[pl.ds(g * group, group)].reshape(side, width)
        done = jnp.dot(third, block, preferred_element_type=jnp.float32)
        done += jnp.dot(second, block, preferred_element_type=jnp.float32)
        done += jnp.dot(first, block, preferred_element_type=jnp.float32)
        done = done.astype(jnp.bfloat16)
        for c in range(2):
            piece = done[:, c * part : (c + 1) * part].reshape(group, rows, part)
            fitted[c, pl.ds(g * group, group)] = piece
        return carry

    lax.fori_loop(0, total_occ // group, fit, 0)

    pl.semaphore_wait(barrier, n - 1)

    def cross_copy(c):
        return pltpu.make_async_remote_copy(
            src_ref=fitted.at[c], dst_ref=crossed[c],
            send_sem=cross_send_sem.at[c], recv_sem=cross_recv_sem.at[c],
            device_id={"aux": across}, device_id_type=pl.DeviceIdType.MESH,
        )

    for c in range(2):
        cross_copy(c).start()

    def block_copy(target, source):
        return pltpu.make_async_remote_copy(
            src_ref=send.at[lax.rem(target, half)], dst_ref=recv.at[source],
            send_sem=send_sem.at[lax.rem(target, half)], recv_sem=recv_sem.at[2, source],
            device_id={"aux": target}, device_id_type=pl.DeviceIdType.MESH,
        )

    def relay_copy(c, target, source):
        return pltpu.make_async_remote_copy(
            src_ref=relay.at[c, lax.rem(target, half)], dst_ref=recv.at[source, c],
            send_sem=relay_sem.at[c, lax.rem(target, half)], recv_sem=recv_sem.at[c, source],
            device_id={"aux": target}, device_id_type=pl.DeviceIdType.MESH,
        )

    def pack(step, carry):
        t = near(step)
        for slot in range(joined):
            one = orbital(t, slot)
            for c in range(2):
                send[lax.rem(t, half), c, slot] = fitted[c, one]
        block_copy(t, me).start()
        return carry

    lax.fori_loop(0, half - 1, pack, 0)
    for slot in range(joined):
        one = orbital(me, slot)
        for c in range(2):
            recv[me, c, slot] = fitted[c, one]

    def hand_on(c):
        cross_copy(c).wait_recv()

        def forward(step, carry):
            t = near(step)
            for slot in range(joined):
                relay[c, lax.rem(t, half), slot] = crossed[c][orbital(t, slot)]
            relay_copy(c, t, across).start()
            return carry

        lax.fori_loop(0, half - 1, forward, 0)
        for slot in range(joined):
            recv[across, c, slot] = crossed[c][orbital(me, slot)]

    depth = table_ref.shape[0]
    n_virt = virt_ref.shape[0]
    full = n_virt // LANES
    table_ref[...] = jnp.zeros_like(table_ref)
    for row in range(full):
        table_ref[row, :] = virt_ref[pl.ds(row * LANES, LANES)]
    if n_virt % LANES:
        table_ref[full, 0 : n_virt % LANES] = virt_ref[pl.ds(full * LANES, n_virt % LANES)]
    by_lane = table_ref[...].T
    for slot in range(joined):
        one = orbital(me, slot)
        index = domains_ref[pl.ds(one, 1), :]
        high = index // LANES
        low = index - high * LANES
        pick = (lax.broadcasted_iota(jnp.int32, (depth, width), 0) == high).astype(jnp.float32)
        values = jnp.dot(by_lane, pick, precision=HIGHEST, preferred_element_type=jnp.float32)
        chosen = jnp.where(lax.broadcasted_iota(jnp.int32, (LANES, width), 0) == low, values, 0.0)
        gaps[pl.ds(slot, 1), :] = jnp.sum(chosen, axis=0, keepdims=True) - occ_ref[one]
    hand_on(0)
    for i in range(slab):
        down = jnp.broadcast_to(gaps[pl.ds(i, 1), :], (width, width)).T

        def invert(j, carry, i=i, down=down):
            inverse[i, j] = 1.0 / (down + gaps[pl.ds(j, 1), :])
            return carry

        lax.fori_loop(0, joined, invert, 0)
    sums[...] = jnp.zeros_like(sums)

    hand_on(1)

    def arrive(step, carry):
        t = near(step)
        block_copy(t, t).wait_recv()
        source = lax.rem(t + half, n)
        for c in range(2):
            relay_copy(c, t, source).wait_recv()
        return carry

    lax.fori_loop(0, half - 1, arrive, 0)

    def whole_block(slot):
        parts = [recv[:, c, slot].reshape(width_p, part) for c in range(2)]
        return jnp.concatenate(parts, axis=1)

    block_of = lax.broadcasted_iota(jnp.int32, (1, width_p), 1) // rows
    for i in range(slab):
        one = orbital(me, i)

        def hit(f, found, one=one):
            return jnp.where(block_of == blocks_ref[f, one], 1.0, found)

        mask = lax.fori_loop(
            0, blocks_ref.shape[0], hit, jnp.zeros((1, width_p), jnp.float32), unroll=width_p <= 512
        )
        turned = whole_block(i).astype(jnp.float32).T
        left_t[i] = (turned * mask).astype(jnp.bfloat16)

    def pairs(i, carry):
        left = left_t[i]
        for j in range(joined):
            right = whole_block(j)
            coulomb = jnp.dot(left, right, preferred_element_type=jnp.float32)
            terms = coulomb * coulomb * inverse[i, j]
            sums[i, pl.ds(j, 1), :] = jnp.sum(terms, axis=0, keepdims=True)
        return carry

    lax.fori_loop(0, slab, pairs, 0)

    ones = jnp.ones((8, width), jnp.float32)
    energies = [
        -lax.dot_general(
            ones, sums[i], (((1,), (1,)), ((), ())),
            precision=HIGHEST, preferred_element_type=jnp.float32,
        )[0:1]
        for i in range(slab)
    ]
    pad = jnp.zeros((8 - slab, LANES), jnp.float32)
    table = jnp.concatenate(energies + [pad], axis=0)
    totals[me] = table

    def total_copy(target, source):
        return pltpu.make_async_remote_copy(
            src_ref=totals.at[me], dst_ref=totals.at[source],
            send_sem=tot_send_sem.at[target], recv_sem=tot_recv_sem.at[source],
            device_id={"aux": target}, device_id_type=pl.DeviceIdType.MESH,
        )

    def give(step, carry):
        total_copy(peer(step), me).start()
        return carry

    lax.fori_loop(0, n - 1, give, 0)

    def take(step, carry):
        source = peer(step)
        total_copy(source, source).wait_recv()
        return carry

    lax.fori_loop(0, n - 1, take, 0)
    whole = jnp.sum(jnp.sum(totals[...], axis=0), axis=(0, 1), keepdims=True) / total_occ
    last = lax.broadcasted_iota(jnp.int32, (8, LANES), 0) == slab
    out_ref[...] = jnp.where(last, whole, table)

    def finish(step, carry):
        t = peer(step)
        total_copy(t, me).wait_send()
        return carry

    lax.fori_loop(0, n - 1, finish, 0)

    def finish_near(step, carry):
        t = near(step)
        block_copy(t, me).wait_send()
        for c in range(2):
            relay_copy(c, t, across).wait_send()
        return carry

    lax.fori_loop(0, half - 1, finish_near, 0)
    for c in range(2):
        cross_copy(c).wait_send()


def split_outputs(table_ref, slab_ref, partner_ref, total_ref):
    slab, npart = partner_ref.shape
    slab_ref[...] = table_ref[0:slab, 0:slab]
    partner_ref[...] = table_ref[0:slab, slab : slab + npart]
    total_ref[...] = table_ref[slab : slab + 1, 0:1]


def per_device(
    three_index, fit_metric, fit_blocks, domains, occ_energy, virt_energy, owner_map, partners
):
    n = lax.axis_size("aux")
    total_occ, rows, width = three_index.shape
    slab = total_occ // n
    npart = partners.shape[1]
    joined = slab + npart
    chunk = 8 * LANES
    depth = -(-virt_energy.shape[0] // chunk) * 8
    smem = pl.BlockSpec(memory_space=pltpu.SMEM)
    vmem = pl.BlockSpec(memory_space=pltpu.VMEM)
    out = pl.pallas_call(
        functools.partial(kernel, n, slab, npart),
        out_shape=jax.ShapeDtypeStruct((8, LANES), jnp.float32),
        in_specs=[smem] * 4 + [vmem] * 4,
        out_specs=vmem,
        scratch_shapes=[
            pltpu.VMEM((2, total_occ, rows, width // 2), jnp.bfloat16),
            pltpu.VMEM((total_occ, rows, width // 2), jnp.bfloat16),
            pltpu.VMEM((total_occ, rows, width // 2), jnp.bfloat16),
            pltpu.VMEM((n // 2, 2, joined, rows, width // 2), jnp.bfloat16),
            pltpu.VMEM((2, n // 2, joined, rows, width // 2), jnp.bfloat16),
            pltpu.VMEM((n, 2, joined, rows, width // 2), jnp.bfloat16),
            pltpu.VMEM((depth, LANES), jnp.float32),
            pltpu.VMEM((slab, joined, width, width), jnp.float32),
            pltpu.VMEM((slab, width, n * rows), jnp.bfloat16),
            pltpu.VMEM((-(-joined // 8) * 8, width), jnp.float32),
            pltpu.VMEM((slab, LANES, width), jnp.float32),
            pltpu.VMEM((n, 8, LANES), jnp.float32),
            pltpu.SemaphoreType.DMA((2,)),
            pltpu.SemaphoreType.DMA((2,)),
            pltpu.SemaphoreType.DMA((n // 2,)),
            pltpu.SemaphoreType.DMA((2, n // 2)),
            pltpu.SemaphoreType.DMA((3, n)),
            pltpu.SemaphoreType.DMA((n,)),
            pltpu.SemaphoreType.DMA((n,)),
        ],
        compiler_params=pltpu.CompilerParams(
            collective_id=0, has_side_effects=True, vmem_limit_bytes=56 * 1024 * 1024
        ),
    )(
        owner_map, partners.T, fit_blocks.T, occ_energy, three_index, fit_metric, domains, virt_energy
    )
    slab_energy, partner_energy, total = pl.pallas_call(
        split_outputs,
        out_shape=(
            jax.ShapeDtypeStruct((slab, slab), jnp.float32),
            jax.ShapeDtypeStruct((slab, npart), jnp.float32),
            jax.ShapeDtypeStruct((1, 1), jnp.float32),
        ),
        in_specs=[vmem],
        out_specs=(vmem, vmem, vmem),
    )(out)
    return slab_energy, partner_energy, total.reshape(1)


def solution(mesh):
    in_specs = (
        P("grp", "aux", None),
        P(("grp", "aux"), None),
        P("grp", None),
        P("grp", None),
        P("grp"),
        P("grp"),
        P("grp"),
        P("grp", None),
    )
    out_specs = (P(("grp", "aux"), None), P(("grp", "aux"), None), P("grp"))
    return jax.shard_map(
        per_device, mesh=mesh, in_specs=in_specs, out_specs=out_specs, check_vma=False
    )
```

```python
import functools

import jax
import jax.numpy as jnp
from jax import lax
from jax.experimental import pallas as pl
from jax.experimental.pallas import tpu as pltpu
from jax.sharding import PartitionSpec as P

HIGHEST = lax.Precision.HIGHEST
LANES = 128


def kernel(
    n, slab, npart,
    owner_ref, partners_ref, blocks_ref, occ_ref,
    three_ref, metric_ref, domains_ref, virt_ref,
    out_ref,
    fitted_a, fitted_b, cross_a, cross_b, send, relay, recv, table_ref, inverse, left_t, gaps, masks, sums, totals,
    cross_send_sem, cross_recv_sem, send_sem, relay_sem, recv_sem, tot_send_sem, tot_recv_sem,
):
    me = lax.axis_index("aux")
    total_occ, rows, width = three_ref.shape
    width_p = n * rows
    joined = slab + npart
    order_start = n // 2 - 1
    half = n // 2
    here = lax.rem(me, half)
    base = me - here
    across = lax.rem(me + half, n)
    crossed = (cross_a, cross_b)
    fitted = (fitted_a, fitted_b)
    part = width // 2

    def near(step):
        return base + lax.rem(here + 1 + step, half)

    def peer(step):
        return lax.rem(me + 1 + lax.rem(step + order_start, n - 1), n)

    def orbital(t, slot):
        return owner_ref[t * slab + slot] if slot < slab else partners_ref[slot - slab, t]

    barrier = pltpu.get_barrier_semaphore()

    def greet(step, carry):
        pl.semaphore_signal(
            barrier, inc=1, device_id={"aux": peer(step)}, device_id_type=pl.DeviceIdType.MESH
        )
        return carry

    lax.fori_loop(0, n - 1, greet, 0)

    group = 256 // rows
    side = group * rows
    tall = jnp.concatenate([metric_ref[...]] * group, axis=0)
    spread = (
        lax.broadcasted_iota(jnp.int32, (rows, side), 1) % rows
        == lax.broadcasted_iota(jnp.int32, (rows, side), 0)
    ).astype(jnp.float32)
    tiled = jnp.dot(tall, spread, precision=HIGHEST, preferred_element_type=jnp.float32)
    same = (
        lax.broadcasted_iota(jnp.int32, (side, side), 0) // rows
        == lax.broadcasted_iota(jnp.int32, (side, side), 1) // rows
    )
    weights = jnp.where(same, tiled, 0.0)
    first = weights.astype(jnp.bfloat16)
    rest = weights - first.astype(jnp.float32)
    second = rest.astype(jnp.bfloat16)
    third = (rest - second.astype(jnp.float32)).astype(jnp.bfloat16)

    def fit_half(c):
        def fit(g, carry):
            block = three_ref[pl.ds(g * group, group), :, c * part : (c + 1) * part].reshape(side, part)
            done = jnp.dot(third, block, preferred_element_type=jnp.float32)
            done += jnp.dot(second, block, preferred_element_type=jnp.float32)
            done += jnp.dot(first, block, preferred_element_type=jnp.float32)
            fitted[c][pl.ds(g * group, group)] = done.astype(jnp.bfloat16).reshape(group, rows, part)
            return carry

        lax.fori_loop(0, total_occ // group, fit, 0)

    fit_half(0)
    pl.semaphore_wait(barrier, n - 1)

    def cross_copy(c):
        return pltpu.make_async_remote_copy(
            src_ref=fitted[c], dst_ref=crossed[c],
            send_sem=cross_send_sem.at[c], recv_sem=cross_recv_sem.at[c],
            device_id={"aux": across}, device_id_type=pl.DeviceIdType.MESH,
        )

    cross_copy(0).start()
    fit_half(1)

    def block_copy(target, source):
        return pltpu.make_async_remote_copy(
            src_ref=send.at[lax.rem(target, half)], dst_ref=recv.at[source],
            send_sem=send_sem.at[lax.rem(target, half)], recv_sem=recv_sem.at[2, source],
            device_id={"aux": target}, device_id_type=pl.DeviceIdType.MESH,
        )

    def relay_copy(c, target, source):
        return pltpu.make_async_remote_copy(
            src_ref=relay.at[c, lax.rem(target, half)], dst_ref=recv.at[source, c],
            send_sem=relay_sem.at[c, lax.rem(target, half)], recv_sem=recv_sem.at[c, source],
            device_id={"aux": target}, device_id_type=pl.DeviceIdType.MESH,
        )

    def pack(step, carry):
        t = near(step)
        for slot in range(joined):
            one = orbital(t, slot)
            for c in range(2):
                send[lax.rem(t, half), c, slot] = fitted[c][one]
        block_copy(t, me).start()
        return carry

    lax.fori_loop(0, half - 1, pack, 0)
    for slot in range(joined):
        one = orbital(me, slot)
        for c in range(2):
            recv[me, c, slot] = fitted[c][one]

    def hand_on(c):
        cross_copy(c).wait_recv()

        def forward(step, carry):
            t = near(step)
            for slot in range(joined):
                relay[c, lax.rem(t, half), slot] = crossed[c][orbital(t, slot)]
            relay_copy(c, t, across).start()
            return carry

        lax.fori_loop(0, half - 1, forward, 0)
        for slot in range(joined):
            recv[across, c, slot] = crossed[c][orbital(me, slot)]

    depth = table_ref.shape[0]
    n_virt = virt_ref.shape[0]
    full = n_virt // LANES
    table_ref[...] = jnp.zeros_like(table_ref)
    for row in range(full):
        table_ref[row, :] = virt_ref[pl.ds(row * LANES, LANES)]
    if n_virt % LANES:
        table_ref[full, 0 : n_virt % LANES] = virt_ref[pl.ds(full * LANES, n_virt % LANES)]
    by_lane = table_ref[...].T
    for slot in range(joined):
        one = orbital(me, slot)
        index = domains_ref[pl.ds(one, 1), :]
        high = index // LANES
        low = index - high * LANES
        pick = (lax.broadcasted_iota(jnp.int32, (depth, width), 0) == high).astype(jnp.float32)
        values = jnp.dot(by_lane, pick, precision=HIGHEST, preferred_element_type=jnp.float32)
        chosen = jnp.where(lax.broadcasted_iota(jnp.int32, (LANES, width), 0) == low, values, 0.0)
        gaps[pl.ds(slot, 1), :] = jnp.sum(chosen, axis=0, keepdims=True) - occ_ref[one]
    cross_copy(0).wait_send()
    cross_copy(1).start()
    hand_on(0)
    for i in range(slab):
        down = jnp.broadcast_to(gaps[pl.ds(i, 1), :], (width, width)).T

        def invert(j, carry, i=i, down=down):
            inverse[i, j] = 1.0 / (down + gaps[pl.ds(j, 1), :])
            return carry

        lax.fori_loop(0, joined, invert, 0)
    sums[...] = jnp.zeros_like(sums)

    block_of = lax.broadcasted_iota(jnp.int32, (1, width_p), 1) // rows
    for i in range(slab):
        one = orbital(me, i)

        def hit(f, found, one=one):
            return jnp.where(block_of == blocks_ref[f, one], 1.0, found)

        masks[pl.ds(i, 1), :] = lax.fori_loop(
            0, blocks_ref.shape[0], hit, jnp.zeros((1, width_p), jnp.float32), unroll=width_p <= 512
        )

    def turn(c):
        for i in range(slab):
            turned = recv[:, c, i].reshape(width_p, part).astype(jnp.float32).T
            left_t[i, c * part : (c + 1) * part] = (turned * masks[pl.ds(i, 1), :]).astype(jnp.bfloat16)

    def arrive_near(step, carry):
        t = near(step)
        block_copy(t, t).wait_recv()
        return carry

    def arrive(c):
        def one_source(step, carry):
            t = near(step)
            relay_copy(c, t, lax.rem(t + half, n)).wait_recv()
            return carry

        lax.fori_loop(0, half - 1, one_source, 0)

    hand_on(1)
    lax.fori_loop(0, half - 1, arrive_near, 0)
    arrive(0)
    turn(0)
    arrive(1)
    turn(1)

    def whole_block(slot):
        parts = [recv[:, c, slot].reshape(width_p, part) for c in range(2)]
        return jnp.concatenate(parts, axis=1)

    def pairs(i, carry):
        left = left_t[i]
        for j in range(joined):
            right = whole_block(j)
            coulomb = jnp.dot(left, right, preferred_element_type=jnp.float32)
            terms = coulomb * coulomb * inverse[i, j]
            sums[i, pl.ds(j, 1), :] = jnp.sum(terms, axis=0, keepdims=True)
        return carry

    lax.fori_loop(0, slab, pairs, 0)

    ones = jnp.ones((8, width), jnp.float32)
    energies = [
        -lax.dot_general(
            ones, sums[i], (((1,), (1,)), ((), ())),
            precision=HIGHEST, preferred_element_type=jnp.float32,
        )[0:1]
        for i in range(slab)
    ]
    pad = jnp.zeros((8 - slab, LANES), jnp.float32)
    table = jnp.concatenate(energies + [pad], axis=0)
    totals[me] = table

    def total_copy(target, source):
        return pltpu.make_async_remote_copy(
            src_ref=totals.at[me], dst_ref=totals.at[source],
            send_sem=tot_send_sem.at[target], recv_sem=tot_recv_sem.at[source],
            device_id={"aux": target}, device_id_type=pl.DeviceIdType.MESH,
        )

    def give(step, carry):
        total_copy(peer(step), me).start()
        return carry

    lax.fori_loop(0, n - 1, give, 0)

    def take(step, carry):
        source = peer(step)
        total_copy(source, source).wait_recv()
        return carry

    lax.fori_loop(0, n - 1, take, 0)
    whole = jnp.sum(jnp.sum(totals[...], axis=0), axis=(0, 1), keepdims=True) / total_occ
    last = lax.broadcasted_iota(jnp.int32, (8, LANES), 0) == slab
    out_ref[...] = jnp.where(last, whole, table)

    def finish(step, carry):
        t = peer(step)
        total_copy(t, me).wait_send()
        return carry

    lax.fori_loop(0, n - 1, finish, 0)

    def finish_near(step, carry):
        t = near(step)
        block_copy(t, me).wait_send()
        for c in range(2):
            relay_copy(c, t, across).wait_send()
        return carry

    lax.fori_loop(0, half - 1, finish_near, 0)
    cross_copy(1).wait_send()


def split_outputs(table_ref, slab_ref, partner_ref, total_ref):
    slab, npart = partner_ref.shape
    slab_ref[...] = table_ref[0:slab, 0:slab]
    partner_ref[...] = table_ref[0:slab, slab : slab + npart]
    total_ref[...] = table_ref[slab : slab + 1, 0:1]


def per_device(
    three_index, fit_metric, fit_blocks, domains, occ_energy, virt_energy, owner_map, partners
):
    n = lax.axis_size("aux")
    total_occ, rows, width = three_index.shape
    slab = total_occ // n
    npart = partners.shape[1]
    joined = slab + npart
    chunk = 8 * LANES
    depth = -(-virt_energy.shape[0] // chunk) * 8
    smem = pl.BlockSpec(memory_space=pltpu.SMEM)
    vmem = pl.BlockSpec(memory_space=pltpu.VMEM)
    out = pl.pallas_call(
        functools.partial(kernel, n, slab, npart),
        out_shape=jax.ShapeDtypeStruct((8, LANES), jnp.float32),
        in_specs=[smem] * 4 + [vmem] * 4,
        out_specs=vmem,
        scratch_shapes=[
            pltpu.VMEM((total_occ, rows, width // 2), jnp.bfloat16),
            pltpu.VMEM((total_occ, rows, width // 2), jnp.bfloat16),
            pltpu.VMEM((total_occ, rows, width // 2), jnp.bfloat16),
            pltpu.VMEM((total_occ, rows, width // 2), jnp.bfloat16),
            pltpu.VMEM((n // 2, 2, joined, rows, width // 2), jnp.bfloat16),
            pltpu.VMEM((2, n // 2, joined, rows, width // 2), jnp.bfloat16),
            pltpu.VMEM((n, 2, joined, rows, width // 2), jnp.bfloat16),
            pltpu.VMEM((depth, LANES), jnp.float32),
            pltpu.VMEM((slab, joined, width, width), jnp.float32),
            pltpu.VMEM((slab, width, n * rows), jnp.bfloat16),
            pltpu.VMEM((-(-joined // 8) * 8, width), jnp.float32),
            pltpu.VMEM((8, n * rows), jnp.float32),
            pltpu.VMEM((slab, LANES, width), jnp.float32),
            pltpu.VMEM((n, 8, LANES), jnp.float32),
            pltpu.SemaphoreType.DMA((2,)),
            pltpu.SemaphoreType.DMA((2,)),
            pltpu.SemaphoreType.DMA((n // 2,)),
            pltpu.SemaphoreType.DMA((2, n // 2)),
            pltpu.SemaphoreType.DMA((3, n)),
            pltpu.SemaphoreType.DMA((n,)),
            pltpu.SemaphoreType.DMA((n,)),
        ],
        compiler_params=pltpu.CompilerParams(
            collective_id=0, has_side_effects=True, vmem_limit_bytes=56 * 1024 * 1024
        ),
    )(
        owner_map, partners.T, fit_blocks.T, occ_energy, three_index, fit_metric, domains, virt_energy
    )
    slab_energy, partner_energy, total = pl.pallas_call(
        split_outputs,
        out_shape=(
            jax.ShapeDtypeStruct((slab, slab), jnp.float32),
            jax.ShapeDtypeStruct((slab, npart), jnp.float32),
            jax.ShapeDtypeStruct((1, 1), jnp.float32),
        ),
        in_specs=[vmem],
        out_specs=(vmem, vmem, vmem),
    )(out)
    return slab_energy, partner_energy, total.reshape(1)


def solution(mesh):
    in_specs = (
        P("grp", "aux", None),
        P(("grp", "aux"), None),
        P("grp", None),
        P("grp", None),
        P("grp"),
        P("grp"),
        P("grp"),
        P("grp", None),
    )
    out_specs = (P(("grp", "aux"), None), P(("grp", "aux"), None), P("grp"))
    return jax.shard_map(
        per_device, mesh=mesh, in_specs=in_specs, out_specs=out_specs, check_vma=False
    )
```

```python
import functools

import jax
import jax.numpy as jnp
from jax import lax
from jax.experimental import pallas as pl
from jax.experimental.pallas import tpu as pltpu
from jax.sharding import PartitionSpec as P

HIGHEST = lax.Precision.HIGHEST
LANES = 128


def kernel(
    n, slab, npart,
    owner_ref, partners_ref, blocks_ref, occ_ref,
    three_ref, metric_ref, domains_ref, virt_ref,
    out_ref,
    fitted_a, fitted_b, cross_a, cross_b, send, relay, recv, table_ref, inverse, left_t, gaps, masks, sums, totals,
    cross_send_sem, cross_recv_sem, send_sem, relay_sem, recv_sem, tot_send_sem, tot_recv_sem,
):
    me = lax.axis_index("aux")
    total_occ, rows, width = three_ref.shape
    width_p = n * rows
    joined = slab + npart
    order_start = n // 2 - 1
    half = n // 2
    quarter = half // 2
    here = lax.rem(me, half)
    base = me - here
    across = lax.rem(me + half, n)
    crossed = (cross_a, cross_b)
    fitted = (fitted_a, fitted_b)
    part = width // 2

    def near(step):
        turn_over = lax.div(step, quarter)
        layer = lax.rem(lax.div(here, quarter) + 1 + turn_over, 2)
        return base + layer * quarter + lax.rem(here + step + turn_over, quarter)

    def peer(step):
        return lax.rem(me + 1 + lax.rem(step + order_start, n - 1), n)

    def orbital(t, slot):
        return owner_ref[t * slab + slot] if slot < slab else partners_ref[slot - slab, t]

    barrier = pltpu.get_barrier_semaphore()

    def greet(step, carry):
        pl.semaphore_signal(
            barrier, inc=1, device_id={"aux": peer(step)}, device_id_type=pl.DeviceIdType.MESH
        )
        return carry

    lax.fori_loop(0, n - 1, greet, 0)

    group = 256 // rows
    side = group * rows
    tall = jnp.concatenate([metric_ref[...]] * group, axis=0)
    spread = (
        lax.broadcasted_iota(jnp.int32, (rows, side), 1) % rows
        == lax.broadcasted_iota(jnp.int32, (rows, side), 0)
    ).astype(jnp.float32)
    tiled = jnp.dot(tall, spread, precision=HIGHEST, preferred_element_type=jnp.float32)
    same = (
        lax.broadcasted_iota(jnp.int32, (side, side), 0) // rows
        == lax.broadcasted_iota(jnp.int32, (side, side), 1) // rows
    )
    weights = jnp.where(same, tiled, 0.0)
    first = weights.astype(jnp.bfloat16)
    rest = weights - first.astype(jnp.float32)
    second = rest.astype(jnp.bfloat16)
    third = (rest - second.astype(jnp.float32)).astype(jnp.bfloat16)

    def fit_half(c):
        def fit(g, carry):
            block = three_ref[pl.ds(g * group, group), :, c * part : (c + 1) * part].reshape(side, part)
            done = jnp.dot(third, block, preferred_element_type=jnp.float32)
            done += jnp.dot(second, block, preferred_element_type=jnp.float32)
            done += jnp.dot(first, block, preferred_element_type=jnp.float32)
            fitted[c][pl.ds(g * group, group)] = done.astype(jnp.bfloat16).reshape(group, rows, part)
            return carry

        lax.fori_loop(0, total_occ // group, fit, 0)

    fit_half(0)
    pl.semaphore_wait(barrier, n - 1)

    def cross_copy(c):
        return pltpu.make_async_remote_copy(
            src_ref=fitted[c], dst_ref=crossed[c],
            send_sem=cross_send_sem.at[c], recv_sem=cross_recv_sem.at[c],
            device_id={"aux": across}, device_id_type=pl.DeviceIdType.MESH,
        )

    cross_copy(0).start()
    fit_half(1)

    def block_copy(target, source):
        return pltpu.make_async_remote_copy(
            src_ref=send.at[lax.rem(target, half)], dst_ref=recv.at[source],
            send_sem=send_sem.at[lax.rem(target, half)], recv_sem=recv_sem.at[2, source],
            device_id={"aux": target}, device_id_type=pl.DeviceIdType.MESH,
        )

    def relay_copy(c, target, source):
        return pltpu.make_async_remote_copy(
            src_ref=relay.at[c, lax.rem(target, half)], dst_ref=recv.at[source, c],
            send_sem=relay_sem.at[c, lax.rem(target, half)], recv_sem=recv_sem.at[c, source],
            device_id={"aux": target}, device_id_type=pl.DeviceIdType.MESH,
        )

    def pack(step, carry):
        t = near(step)
        for slot in range(joined):
            one = orbital(t, slot)
            for c in range(2):
                send[lax.rem(t, half), c, slot] = fitted[c][one]
        block_copy(t, me).start()
        return carry

    lax.fori_loop(0, half - 1, pack, 0)
    for slot in range(joined):
        one = orbital(me, slot)
        for c in range(2):
            recv[me, c, slot] = fitted[c][one]

    def hand_on(c):
        cross_copy(c).wait_recv()

        def forward(step, carry):
            t = near(step)
            for slot in range(joined):
                relay[c, lax.rem(t, half), slot] = crossed[c][orbital(t, slot)]
            relay_copy(c, t, across).start()
            return carry

        lax.fori_loop(0, half - 1, forward, 0)
        for slot in range(joined):
            recv[across, c, slot] = crossed[c][orbital(me, slot)]

    depth = table_ref.shape[0]
    n_virt = virt_ref.shape[0]
    full = n_virt // LANES
    table_ref[...] = jnp.zeros_like(table_ref)
    for row in range(full):
        table_ref[row, :] = virt_ref[pl.ds(row * LANES, LANES)]
    if n_virt % LANES:
        table_ref[full, 0 : n_virt % LANES] = virt_ref[pl.ds(full * LANES, n_virt % LANES)]
    by_lane = table_ref[...].T
    for slot in range(joined):
        one = orbital(me, slot)
        index = domains_ref[pl.ds(one, 1), :]
        high = index // LANES
        low = index - high * LANES
        pick = (lax.broadcasted_iota(jnp.int32, (depth, width), 0) == high).astype(jnp.float32)
        values = jnp.dot(by_lane, pick, precision=HIGHEST, preferred_element_type=jnp.float32)
        chosen = jnp.where(lax.broadcasted_iota(jnp.int32, (LANES, width), 0) == low, values, 0.0)
        gaps[pl.ds(slot, 1), :] = jnp.sum(chosen, axis=0, keepdims=True) - occ_ref[one]
    cross_copy(0).wait_send()
    cross_copy(1).start()
    hand_on(0)
    for i in range(slab):
        down = jnp.broadcast_to(gaps[pl.ds(i, 1), :], (width, width)).T

        def invert(j, carry, i=i, down=down):
            inverse[i, j] = 1.0 / (down + gaps[pl.ds(j, 1), :])
            return carry

        lax.fori_loop(0, joined, invert, 0)
    sums[...] = jnp.zeros_like(sums)

    block_of = lax.broadcasted_iota(jnp.int32, (1, width_p), 1) // rows
    for i in range(slab):
        one = orbital(me, i)

        def hit(f, found, one=one):
            return jnp.where(block_of == blocks_ref[f, one], 1.0, found)

        masks[pl.ds(i, 1), :] = lax.fori_loop(
            0, blocks_ref.shape[0], hit, jnp.zeros((1, width_p), jnp.float32), unroll=width_p <= 512
        )

    def turn(c):
        for i in range(slab):
            turned = recv[:, c, i].reshape(width_p, part).astype(jnp.float32).T
            left_t[i, c * part : (c + 1) * part] = (turned * masks[pl.ds(i, 1), :]).astype(jnp.bfloat16)

    def arrive_near(step, carry):
        t = near(step)
        block_copy(t, t).wait_recv()
        return carry

    def arrive(c):
        def one_source(step, carry):
            t = near(step)
            relay_copy(c, t, lax.rem(t + half, n)).wait_recv()
            return carry

        lax.fori_loop(0, half - 1, one_source, 0)

    hand_on(1)
    lax.fori_loop(0, half - 1, arrive_near, 0)
    arrive(0)
    turn(0)
    arrive(1)
    turn(1)

    def whole_block(slot):
        parts = [recv[:, c, slot].reshape(width_p, part) for c in range(2)]
        return jnp.concatenate(parts, axis=1)

    def pairs(i, carry):
        left = left_t[i]
        for j in range(joined):
            right = whole_block(j)
            coulomb = jnp.dot(left, right, preferred_element_type=jnp.float32)
            terms = coulomb * coulomb * inverse[i, j]
            sums[i, pl.ds(j, 1), :] = jnp.sum(terms, axis=0, keepdims=True)
        return carry

    lax.fori_loop(0, slab, pairs, 0)

    ones = jnp.ones((8, width), jnp.float32)
    energies = [
        -lax.dot_general(
            ones, sums[i], (((1,), (1,)), ((), ())),
            precision=HIGHEST, preferred_element_type=jnp.float32,
        )[0:1]
        for i in range(slab)
    ]
    pad = jnp.zeros((8 - slab, LANES), jnp.float32)
    table = jnp.concatenate(energies + [pad], axis=0)
    totals[me] = table

    def total_copy(target, source):
        return pltpu.make_async_remote_copy(
            src_ref=totals.at[me], dst_ref=totals.at[source],
            send_sem=tot_send_sem.at[target], recv_sem=tot_recv_sem.at[source],
            device_id={"aux": target}, device_id_type=pl.DeviceIdType.MESH,
        )

    def give(step, carry):
        total_copy(peer(step), me).start()
        return carry

    lax.fori_loop(0, n - 1, give, 0)

    def take(step, carry):
        source = peer(step)
        total_copy(source, source).wait_recv()
        return carry

    lax.fori_loop(0, n - 1, take, 0)
    whole = jnp.sum(jnp.sum(totals[...], axis=0), axis=(0, 1), keepdims=True) / total_occ
    last = lax.broadcasted_iota(jnp.int32, (8, LANES), 0) == slab
    out_ref[...] = jnp.where(last, whole, table)

    def finish(step, carry):
        t = peer(step)
        total_copy(t, me).wait_send()
        return carry

    lax.fori_loop(0, n - 1, finish, 0)

    def finish_near(step, carry):
        t = near(step)
        block_copy(t, me).wait_send()
        for c in range(2):
            relay_copy(c, t, across).wait_send()
        return carry

    lax.fori_loop(0, half - 1, finish_near, 0)
    cross_copy(1).wait_send()


def split_outputs(table_ref, slab_ref, partner_ref, total_ref):
    slab, npart = partner_ref.shape
    slab_ref[...] = table_ref[0:slab, 0:slab]
    partner_ref[...] = table_ref[0:slab, slab : slab + npart]
    total_ref[...] = table_ref[slab : slab + 1, 0:1]


def per_device(
    three_index, fit_metric, fit_blocks, domains, occ_energy, virt_energy, owner_map, partners
):
    n = lax.axis_size("aux")
    total_occ, rows, width = three_index.shape
    slab = total_occ // n
    npart = partners.shape[1]
    joined = slab + npart
    chunk = 8 * LANES
    depth = -(-virt_energy.shape[0] // chunk) * 8
    smem = pl.BlockSpec(memory_space=pltpu.SMEM)
    vmem = pl.BlockSpec(memory_space=pltpu.VMEM)
    out = pl.pallas_call(
        functools.partial(kernel, n, slab, npart),
        out_shape=jax.ShapeDtypeStruct((8, LANES), jnp.float32),
        in_specs=[smem] * 4 + [vmem] * 4,
        out_specs=vmem,
        scratch_shapes=[
            pltpu.VMEM((total_occ, rows, width // 2), jnp.bfloat16),
            pltpu.VMEM((total_occ, rows, width // 2), jnp.bfloat16),
            pltpu.VMEM((total_occ, rows, width // 2), jnp.bfloat16),
            pltpu.VMEM((total_occ, rows, width // 2), jnp.bfloat16),
            pltpu.VMEM((n // 2, 2, joined, rows, width // 2), jnp.bfloat16),
            pltpu.VMEM((2, n // 2, joined, rows, width // 2), jnp.bfloat16),
            pltpu.VMEM((n, 2, joined, rows, width // 2), jnp.bfloat16),
            pltpu.VMEM((depth, LANES), jnp.float32),
            pltpu.VMEM((slab, joined, width, width), jnp.float32),
            pltpu.VMEM((slab, width, n * rows), jnp.bfloat16),
            pltpu.VMEM((-(-joined // 8) * 8, width), jnp.float32),
            pltpu.VMEM((8, n * rows), jnp.float32),
            pltpu.VMEM((slab, LANES, width), jnp.float32),
            pltpu.VMEM((n, 8, LANES), jnp.float32),
            pltpu.SemaphoreType.DMA((2,)),
            pltpu.SemaphoreType.DMA((2,)),
            pltpu.SemaphoreType.DMA((n // 2,)),
            pltpu.SemaphoreType.DMA((2, n // 2)),
            pltpu.SemaphoreType.DMA((3, n)),
            pltpu.SemaphoreType.DMA((n,)),
            pltpu.SemaphoreType.DMA((n,)),
        ],
        compiler_params=pltpu.CompilerParams(
            collective_id=0, has_side_effects=True, vmem_limit_bytes=56 * 1024 * 1024
        ),
    )(
        owner_map, partners.T, fit_blocks.T, occ_energy, three_index, fit_metric, domains, virt_energy
    )
    slab_energy, partner_energy, total = pl.pallas_call(
        split_outputs,
        out_shape=(
            jax.ShapeDtypeStruct((slab, slab), jnp.float32),
            jax.ShapeDtypeStruct((slab, npart), jnp.float32),
            jax.ShapeDtypeStruct((1, 1), jnp.float32),
        ),
        in_specs=[vmem],
        out_specs=(vmem, vmem, vmem),
    )(out)
    return slab_energy, partner_energy, total.reshape(1)


def solution(mesh):
    in_specs = (
        P("grp", "aux", None),
        P(("grp", "aux"), None),
        P("grp", None),
        P("grp", None),
        P("grp"),
        P("grp"),
        P("grp"),
        P("grp", None),
    )
    out_specs = (P(("grp", "aux"), None), P(("grp", "aux"), None), P("grp"))
    return jax.shard_map(
        per_device, mesh=mesh, in_specs=in_specs, out_specs=out_specs, check_vma=False
    )
```
